32 devices in a mesh: groups: 2 (over y), space: 4 (over z), phase: 4 (over x, core).
Axes of the slice: x: 2, y: 2, z: 4, core: 2. Of those that a mesh axis runs over, the one named last changes fastest.
Arguments:
- intensity: float32 [16, 131072], P('phase', ('groups', 'space')), parts along dimension 1, may hold values from -6 to 6
- image_grad: bfloat16 [3, 16, 131072], P(None, 'phase', ('groups', 'space')), parts along dimension 2, may hold values from -6 to 6
- owner: int32 [131072, 1], P(('groups', 'space')), parts along dimension 0, may hold values from 0 to 3; in each aligned block of 16384 rows (0 to 16383, 16384 to 32767, ...) at most 8192 rows name the same one
- coord_xy: int32 [2, 131072], P(None, ('groups', 'space')), parts along dimension 1, may hold values from 0 to 463
- coord_z: int32 [131072], P(('groups', 'space')), parts along dimension 0, may hold values from 0 to 127
Outputs:
- control_grad: float32 [6, 16, 32, 1024], P('groups', 'phase', 'space'), parts along dimension 0
The draws below stay inside these ranges and needn't reach their ends.
There are 2 independent parts, one for each index of `groups`. The reference program is written for one: setup_inputs(seed, part) draws one part's arguments, and reference() takes and returns one part's arrays. A program takes and returns all parts, laid end to end along the dimension named above; each array names one. Nothing has to cross between parts.
Inputs may be any that keep to these rules, and one draw needn't show every extreme that they name: Of the samples of one device, at most 8192 name the same owner, and some device has exactly 8192 samples for some owner.
All inputs are finite; a program needn't handle non-finite values.
Results may differ from the reference program's by a relative error of at most 0.0041.
Values sent between devices are 32-bit elements; how exact they have to be, the bound alone decides.
A program may use at most 64 MiB of HBM per device.

```python
import math
import jax
import jax.numpy as jnp
import numpy as np
from jax import lax

P_SIZE = 16
GX = 32
SPC = 16
GZ_DEV = 8
S_DEV = 16384
CAP = 8192
NSAMP = 65536
NZC = 32
N_SPACE = 4


def set_ends(result, stream_key, low, high):
    longest = result.shape.index(max(result.shape))
    spots = []
    for shift in (0, 1):
        where = [jax.random.randint(jax.random.fold_in(stream_key, axis), (), 0, length) for axis, length in enumerate(result.shape)]
        where[longest] = (where[longest] + shift) % result.shape[longest]
        spots.append(tuple(where))
    return result.at[spots[0]].set(low).at[spots[1]].set(high)


def levels(rng, dims, split, smallest, high):
    level, own = 1.0, jax.random.fold_in(rng, 6)
    for dim, shards_of in split:
        steps = jnp.exp(jax.random.uniform(jax.random.fold_in(own, dim), (shards_of,), jnp.float32, smallest / len(split), high / len(split)))
        level = level * jnp.repeat(steps, dims[dim] // shards_of).reshape([-1 if axis == dim else 1 for axis in range(len(dims))])
    return level


def routed_block(rng, own, number, rows, amount, top, bound, skew):
    sequence = jax.random.permutation(rng, amount)
    crowded, usual = portions_of(amount, rows * top, bound, skew, True), portions_of(amount, rows * top, bound, skew, False)
    places = jnp.arange(amount)

    def named(sizes, rotation):
        used = int((sizes > 0).sum())
        fixed = max(1, used // 4)
        moved = fixed + (places - fixed + rotation * (used - fixed)) % max(1, amount - fixed)
        return jnp.zeros((amount,), jnp.int32).at[sequence[jnp.where(places < fixed, places, moved)]].set(jnp.asarray(sizes, jnp.int32))

    sizes = jnp.where(number % 4 == 0, named(crowded, number // 4), named(usual, number - number // 4 - 1))
    mixed = jax.random.permutation(jax.random.fold_in(own, 3), amount)
    giver, taker = mixed[0:amount // 2 * 2:2], mixed[1:amount // 2 * 2:2]
    margin = jnp.minimum(sizes[giver] - 1, bound - sizes[taker]) // 2
    margin = jnp.where((giver == sequence[0]) | (taker == sequence[0]) | (sizes[taker] == 0), 0, jnp.maximum(margin, 0))
    moved = jax.random.randint(jax.random.fold_in(own, 4), (amount // 2,), 0, 1 << 20) % (margin + 1)
    sizes = sizes.at[giver].add(-moved).at[taker].add(moved)
    labels = jnp.searchsorted(jnp.cumsum(sizes), jnp.arange(rows * top), side="right").astype(jnp.int32)
    listing = labels.reshape(top, rows).T
    listing = listing[jax.random.permutation(jax.random.fold_in(own, 1), rows)]
    rotation = jax.random.randint(jax.random.fold_in(own, 2), (rows, 1), 0, top)
    return jnp.take_along_axis(listing, (jnp.arange(top)[None, :] + rotation) % top, axis=1)


def portions_of(number_of, total, reach, skew, full):
    weights = [(1 << 20) // math.isqrt(rank ** skew) + 1 for rank in range(1, number_of + 1)]
    largest = reach if full else min(reach, max(-(-total // number_of), total * weights[0] // sum(weights)))
    least = 1 if total - largest >= number_of - 1 else 0
    holding, surplus = [largest] + [least] * (number_of - 1), total - largest - least * (number_of - 1)
    while surplus > 0:
        free = [i for i in range(1, number_of) if holding[i] < largest] or [i for i in range(1, number_of) if holding[i] < reach]
        pool, left = sum([weights[i] for i in free]), surplus
        for i in free:
            more = min(reach - holding[i], max(1, left * weights[i] // pool), surplus)
            holding[i] = holding[i] + more
            surplus = surplus - more
    return np.array(holding)


def gaussian(rng, shape, scale, bound, shards=(), kind=jnp.bfloat16):
    level = levels(rng, shape, shards, -0.22, 0.18) if shards else 1.0
    entries = jax.random.normal(rng, shape, jnp.float32) * scale * level
    return jnp.minimum(jnp.maximum(entries, -bound), bound).astype(kind)


def setup_inputs(seed: int = 0, part: int = 0) -> dict:
    seeds = jax.random.split(jax.random.key(seed), 6)
    part_splits = jax.random.split(jax.random.fold_in(seeds[5], part), 6)
    intensity = gaussian(part_splits[0], (P_SIZE, NSAMP), 1.0, 6.0, ((0, 4), (1, 4)), jnp.float32)
    image_grad = gaussian(part_splits[1], (3, P_SIZE, NSAMP), 1.0, 6.0, ((1, 4), (2, 4)))
    owner_keys = jax.random.split(jax.random.fold_in(part_splits[2], 1), NSAMP // S_DEV)
    owner_turns = jax.random.permutation(jax.random.fold_in(part_splits[2], 3), NSAMP // S_DEV)
    owner = jax.vmap(lambda own, number: routed_block(jax.random.fold_in(part_splits[2], 2), own, number, S_DEV, N_SPACE, 1, CAP, 2))(owner_keys, owner_turns).reshape((NSAMP, 1))
    coord_xy = set_ends(jax.random.randint(part_splits[3], (2, NSAMP), 0, (GX - 3) * SPC), jax.random.fold_in(part_splits[3], 1), 0, ((GX - 3) * SPC) - 1).astype(jnp.int32)
    coord_z = set_ends(jax.random.randint(part_splits[4], (NSAMP,), 0, GZ_DEV * SPC), jax.random.fold_in(part_splits[4], 1), 0, (GZ_DEV * SPC) - 1).astype(jnp.int32)
    return dict(intensity=intensity, image_grad=image_grad, owner=owner, coord_xy=coord_xy, coord_z=coord_z)


def spline_values(offset):
    square = offset * offset
    cube = square * offset
    remain = 1.0 - offset
    return (remain * remain * remain / 6.0, (3.0 * cube - 6.0 * square + 4.0) / 6.0, (-3.0 * cube + 3.0 * square + 3.0 * offset + 1.0) / 6.0, cube / 6.0)

def reference(intensity, image_grad, owner, coord_xy, coord_z):
    samples = intensity.shape[1]
    phase_mean = lax.optimization_barrier(jnp.mean(intensity, axis=0))
    centered = intensity - phase_mean
    phase_var = lax.optimization_barrier(jnp.mean(centered * centered, axis=0))
    deviation = 2.0 * centered / jnp.sqrt(phase_var + 1.0)
    forces = (deviation[None] * image_grad.astype(jnp.float32)).reshape(3 * P_SIZE, samples)
    pos_x = coord_xy[0].astype(jnp.float32) / SPC
    pos_y = coord_xy[1].astype(jnp.float32) / SPC
    pos_z = coord_z.astype(jnp.float32) / SPC
    floor_x = jnp.floor(pos_x)
    floor_y = jnp.floor(pos_y)
    floor_z = jnp.floor(pos_z)
    offset_x = pos_x - floor_x
    offset_y = pos_y - floor_y
    offset_z = pos_z - floor_z
    corner_x = floor_x.astype(jnp.int32)
    corner_y = floor_y.astype(jnp.int32)
    corner_z = owner[:, 0].astype(jnp.int32) * GZ_DEV + floor_z.astype(jnp.int32)
    block_rows = min(4096, samples)
    block_count = samples // block_rows
    cells = (NZC + 3) * GX * GX
    steps_four = jnp.arange(4, dtype=jnp.int32)

    def accumulate(block_id, grid):
        start = (block_id * block_rows).astype(jnp.int32)

        def pick(array):
            return lax.dynamic_slice_in_dim(array, start, block_rows, array.ndim - 1)
        vals_x = jnp.stack(spline_values(pick(offset_x)), axis=1)
        vals_y = jnp.stack(spline_values(pick(offset_y)), axis=1)
        vals_z = jnp.stack(spline_values(pick(offset_z)), axis=1)
        force_rows = pick(forces)
        lifted = force_rows[:, None, :] * vals_z.T[None, :, :]
        lifted = lax.optimization_barrier(lifted.astype(jnp.bfloat16)).astype(jnp.float32)
        plane = vals_x[:, :, None] * vals_y[:, None, :]
        plane = lax.optimization_barrier(plane.astype(jnp.bfloat16)).astype(jnp.float32)
        contrib = jnp.transpose(lifted, (2, 1, 0))[:, :, None, None, :] * plane[:, None, :, :, None]
        rows_z = pick(corner_z)[:, None] + steps_four[None, :]
        rows_x = pick(corner_x)[:, None] + steps_four[None, :]
        rows_y = pick(corner_y)[:, None] + steps_four[None, :]
        index = (rows_z[:, :, None, None] * GX + rows_x[:, None, :, None]) * GX + rows_y[:, None, None, :]
        return grid.at[index.reshape(-1)].add(contrib.reshape(-1, 3 * P_SIZE))
    grid = lax.fori_loop(0, block_count, accumulate, jnp.zeros((cells, 3 * P_SIZE), jnp.float32))
    kept = grid[:NZC * GX * GX].reshape(NZC, GX * GX, 3, P_SIZE)
    return jnp.transpose(kept, (2, 3, 0, 1))
```

```python
import functools

import jax
import jax.numpy as jnp
from jax import lax
from jax.experimental import pallas as pl
from jax.experimental.pallas import tpu as pltpu
from jax.sharding import PartitionSpec as P

GX = 32
SPC = 16
GZ_DEV = 8
X_STEP = 8
MESH = pl.DeviceIdType.MESH


def spline_values(offset):
    square = offset * offset
    cube = square * offset
    remain = 1.0 - offset
    sixth = 1.0 / 6.0
    return (
        remain * remain * remain * sixth,
        (3.0 * cube - 6.0 * square + 4.0) * sixth,
        (-3.0 * cube + 3.0 * square + 3.0 * offset + 1.0) * sixth,
        cube * sixth,
    )


def spread(corner, offset, first, extent):
    width = corner.shape[1]
    row = first + lax.broadcasted_iota(jnp.int32, (extent, width), 0)
    distance = row - corner
    weights = jnp.zeros((extent, width), jnp.float32)
    for which, value in enumerate(spline_values(offset)):
        weights = jnp.where(distance == which, value, weights)
    return weights


def split_coord(coord):
    corner = coord // SPC
    return corner, (coord - corner * SPC).astype(jnp.float32) * (1.0 / SPC)


def kernel(
    n_space, n_phase, step,
    inten_ref, grad_ref, owner_ref, xy_ref, z_ref, out_ref,
    stat, heard, wx, wy, forces, lifted, acc, from_low, from_high,
    stat_send, stat_recv, up_send, up_recv, down_send, down_recv,
):
    ph_dev, samples = inten_ref.shape
    count = samples // step
    rows = 3 * ph_dev * GZ_DEV
    chunks = GX // X_STEP
    cols = X_STEP * GX
    rounds = n_phase.bit_length() - 1
    me = lax.axis_index("space")
    ph = lax.axis_index("phase")
    partners = [ph + (1 - 2 * ((ph // (1 << r)) % 2)) * (1 << r) for r in range(rounds)]

    barrier = pltpu.get_barrier_semaphore()
    for partner in partners:
        pl.semaphore_signal(barrier, inc=1, device_id={"phase": partner}, device_id_type=MESH)

    @pl.when(me > 0)
    def _():
        pl.semaphore_signal(barrier, inc=1, device_id={"space": me - 1}, device_id_type=MESH)

    @pl.when(me < n_space - 1)
    def _():
        pl.semaphore_signal(barrier, inc=1, device_id={"space": me + 1}, device_id_type=MESH)

    def ks(k):
        return pl.ds(pl.multiple_of(k * step, step), step)

    def local_stats(k, carry):
        block = inten_ref[:, ks(k)]
        mean = jnp.sum(block, axis=0, keepdims=True) * (1.0 / ph_dev)
        centered = block - mean
        stat[0, 0:1, ks(k)] = mean
        stat[0, 1:2, ks(k)] = jnp.sum(centered * centered, axis=0, keepdims=True)
        return carry

    lax.fori_loop(0, count, local_stats, 0)

    neighbours = jnp.where(me > 0, 1, 0) + jnp.where(me < n_space - 1, 1, 0)
    pl.semaphore_wait(barrier, rounds + neighbours)

    def plane_weights(k, carry):
        for axis, weights in ((0, wx), (1, wy)):
            corner, offset = split_coord(xy_ref[axis:axis + 1, ks(k)])
            weights[:, ks(k)] = spread(corner, offset, 0, GX)
        return carry

    for r in range(rounds):
        copy = pltpu.make_async_remote_copy(
            src_ref=stat.at[r],
            dst_ref=heard.at[r],
            send_sem=stat_send.at[r],
            recv_sem=stat_recv.at[r],
            device_id={"phase": partners[r]},
            device_id_type=MESH,
        )
        copy.start()
        lax.fori_loop(count * r // rounds, count * (r + 1) // rounds, plane_weights, 0)
        copy.wait()
        half = 0.5 * (ph_dev << r)

        def join(k, carry, r=r, half=half):
            apart = stat[r, 0:1, ks(k)] - heard[r, 0:1, ks(k)]
            stat[r + 1, 0:1, ks(k)] = 0.5 * (stat[r, 0:1, ks(k)] + heard[r, 0:1, ks(k)])
            stat[r + 1, 1:2, ks(k)] = (
                stat[r, 1:2, ks(k)] + heard[r, 1:2, ks(k)] + half * (apart * apart)
            )
            return carry

        lax.fori_loop(0, count, join, 0)

    def lift(k, carry):
        mean = stat[rounds, 0:1, ks(k)]
        var = stat[rounds, 1:2, ks(k)] * (1.0 / (ph_dev * n_phase))
        deviation = (inten_ref[:, ks(k)] - mean) * (2.0 * lax.rsqrt(var + 1.0))
        for c in range(3):
            forces[c * ph_dev:(c + 1) * ph_dev, :] = deviation * grad_ref[c, :, ks(k)].astype(
                jnp.float32
            )
        corner, offset = split_coord(z_ref[:, ks(k)])
        corner = corner + owner_ref[:, ks(k)] * GZ_DEV
        for o in range(n_space):
            along_z = spread(corner, offset, o * GZ_DEV, GZ_DEV)
            for pair in range(3 * ph_dev // 2):
                both = jnp.concatenate(
                    [
                        forces[2 * pair:2 * pair + 1, :] * along_z,
                        forces[2 * pair + 1:2 * pair + 2, :] * along_z,
                    ],
                    axis=0,
                )
                at = o * rows + 2 * pair * GZ_DEV
                lifted[at:at + 2 * GZ_DEV, ks(k)] = both.astype(jnp.bfloat16)
        return carry

    lax.fori_loop(0, count, lift, 0)

    def up_copy(c, j):
        return pltpu.make_async_remote_copy(
            src_ref=acc.at[c, n_space - 1 - j],
            dst_ref=from_low.at[c, j],
            send_sem=up_send.at[c, j],
            recv_sem=up_recv.at[c, j],
            device_id={"space": me + 1},
            device_id_type=MESH,
        )

    def down_copy(c, j):
        return pltpu.make_async_remote_copy(
            src_ref=acc.at[c, j],
            dst_ref=from_high.at[c, j],
            send_sem=down_send.at[c, j],
            recv_sem=down_recv.at[c, j],
            device_id={"space": me - 1},
            device_id_type=MESH,
        )

    def forward_up(c):
        def one(j, carry):
            target = n_space - 1 - j

            @pl.when((me > 0) & (me <= target))
            def _():
                up_copy(c, j).wait_recv()

            @pl.when((me > 0) & (me < target))
            def _():
                acc[c, target] += from_low[c, j]

            @pl.when(me < target)
            def _():
                up_copy(c, j).start()

            return carry

        lax.fori_loop(0, n_space - 1, one, 0)

    def forward_down(c):
        def one(j, carry):
            @pl.when((me < n_space - 1) & (me >= j))
            def _():
                down_copy(c, j).wait_recv()

            @pl.when((me < n_space - 1) & (me > j))
            def _():
                acc[c, j] += from_high[c, j]

            @pl.when(me > j)
            def _():
                down_copy(c, j).start()

            return carry

        lax.fori_loop(0, n_space - 1, one, 0)

    def slot(t, carry):
        @pl.when(t < chunks)
        def _():
            acc[t] = jnp.zeros(acc.shape[1:], jnp.float32)

            def multiply(k, inner):
                along_y = wy[:, ks(k)]
                along_x = wx[pl.ds(pl.multiple_of(t * X_STEP, X_STEP), X_STEP), ks(k)]
                plane = jnp.concatenate(
                    [(along_x[i:i + 1] * along_y).astype(jnp.bfloat16) for i in range(X_STEP)],
                    axis=0,
                )
                part = lax.dot_general(
                    lifted[:, ks(k)], plane, (((1,), (1,)), ((), ())),
                    preferred_element_type=jnp.float32,
                )
                acc[t] += part.reshape(n_space, rows, cols)
                return inner

            lax.fori_loop(0, count, multiply, 0)

        c_up = t - me
        c_down = t - (n_space - 1 - me)

        @pl.when((c_up >= 0) & (c_up < chunks))
        def _():
            forward_up(c_up)

        @pl.when((c_down >= 0) & (c_down < chunks))
        def _():
            forward_down(c_down)

        return carry

    lax.fori_loop(0, chunks + n_space - 1, slot, 0)

    for c in range(chunks):
        out_ref[:, c * cols:(c + 1) * cols] = acc[c, me]

        @pl.when(me > 0)
        def _():
            out_ref[:, c * cols:(c + 1) * cols] += from_low[c, n_space - 1 - me]

        @pl.when(me < n_space - 1)
        def _():
            out_ref[:, c * cols:(c + 1) * cols] += from_high[c, me]

    def drain(j, carry):
        for c in range(chunks):
            @pl.when(me < n_space - 1 - j)
            def _():
                up_copy(c, j).wait_send()

            @pl.when(me > j)
            def _():
                down_copy(c, j).wait_send()

        return carry

    lax.fori_loop(0, n_space - 1, drain, 0)


def local(intensity, image_grad, owner, coord_xy, coord_z):
    ph_dev, samples = intensity.shape
    n_space = lax.axis_size("space")
    n_phase = lax.axis_size("phase")
    step = min(1024, samples)
    rows = 3 * ph_dev * GZ_DEV
    chunks = GX // X_STEP
    cols = X_STEP * GX
    rounds = n_phase.bit_length() - 1
    hops = n_space - 1
    dma = pltpu.SemaphoreType.DMA
    out = pl.pallas_call(
        functools.partial(kernel, n_space, n_phase, step),
        out_shape=jax.ShapeDtypeStruct((rows, GX * GX), jnp.float32),
        in_specs=[pl.BlockSpec(memory_space=pltpu.VMEM)] * 5,
        out_specs=pl.BlockSpec(memory_space=pltpu.VMEM),
        scratch_shapes=[
            pltpu.VMEM((rounds + 1, 2, samples), jnp.float32),
            pltpu.VMEM((rounds, 2, samples), jnp.float32),
            pltpu.VMEM((GX, samples), jnp.float32),
            pltpu.VMEM((GX, samples), jnp.float32),
            pltpu.VMEM((3 * ph_dev, step), jnp.float32),
            pltpu.VMEM((n_space * rows, samples), jnp.bfloat16),
            pltpu.VMEM((chunks, n_space, rows, cols), jnp.float32),
            pltpu.VMEM((chunks, hops, rows, cols), jnp.float32),
            pltpu.VMEM((chunks, hops, rows, cols), jnp.float32),
            dma((rounds,)),
            dma((rounds,)),
            dma((chunks, hops)),
            dma((chunks, hops)),
            dma((chunks, hops)),
            dma((chunks, hops)),
        ],
        compiler_params=pltpu.CompilerParams(
            collective_id=0, has_side_effects=True, vmem_limit_bytes=58 * 1024 * 1024
        ),
    )(
        intensity,
        image_grad,
        owner.reshape(1, samples),
        coord_xy,
        coord_z.reshape(1, samples),
    )
    return out.reshape(3, ph_dev, GZ_DEV, GX * GX)


def solution(mesh):
    return jax.shard_map(
        local,
        mesh=mesh,
        in_specs=(
            P("phase", ("groups", "space")),
            P(None, "phase", ("groups", "space")),
            P(("groups", "space"), None),
            P(None, ("groups", "space")),
            P(("groups", "space")),
        ),
        out_specs=P("groups", "phase", "space", None),
        check_vma=False,
    )
```

```python
import functools

import jax
import jax.numpy as jnp
from jax import lax
from jax.experimental import pallas as pl
from jax.experimental.pallas import tpu as pltpu
from jax.sharding import PartitionSpec as P

GX = 32
SPC = 16
GZ_DEV = 8
X_STEP = 8
MESH = pl.DeviceIdType.MESH


def spline_values(offset):
    square = offset * offset
    cube = square * offset
    remain = 1.0 - offset
    sixth = 1.0 / 6.0
    return (
        remain * remain * remain * sixth,
        (3.0 * cube - 6.0 * square + 4.0) * sixth,
        (-3.0 * cube + 3.0 * square + 3.0 * offset + 1.0) * sixth,
        cube * sixth,
    )


def spread(corner, offset, first, extent):
    width = corner.shape[1]
    row = first + lax.broadcasted_iota(jnp.int32, (extent, width), 0)
    distance = row - corner
    weights = jnp.zeros((extent, width), jnp.float32)
    for which, value in enumerate(spline_values(offset)):
        weights = jnp.where(distance == which, value, weights)
    return weights


def split_coord(coord):
    corner = coord // SPC
    return corner, (coord - corner * SPC).astype(jnp.float32) * (1.0 / SPC)


def kernel(
    n_space, n_phase, step,
    inten_ref, grad_ref, owner_ref, xy_ref, z_ref, out_ref,
    stat, heard, wx, wy, forces, lifted, acc, from_low, from_high,
    stat_send, stat_recv, up_send, up_recv, down_send, down_recv,
):
    ph_dev, samples = inten_ref.shape
    count = samples // step
    rows = 3 * ph_dev * GZ_DEV
    chunks = GX // X_STEP
    cols = X_STEP * GX
    rounds = n_phase.bit_length() - 1
    me = lax.axis_index("space")
    ph = lax.axis_index("phase")
    partners = [ph + (1 - 2 * ((ph // (1 << r)) % 2)) * (1 << r) for r in range(rounds)]

    barrier = pltpu.get_barrier_semaphore()
    for partner in partners:
        pl.semaphore_signal(barrier, inc=1, device_id={"phase": partner}, device_id_type=MESH)

    @pl.when(me > 0)
    def _():
        pl.semaphore_signal(barrier, inc=1, device_id={"space": me - 1}, device_id_type=MESH)

    @pl.when(me < n_space - 1)
    def _():
        pl.semaphore_signal(barrier, inc=1, device_id={"space": me + 1}, device_id_type=MESH)

    def ks(k):
        return pl.ds(pl.multiple_of(k * step, step), step)

    mstep = min(4096, samples)

    def mk(k):
        return pl.ds(pl.multiple_of(k * mstep, mstep), mstep)

    def local_stats(k, carry):
        block = inten_ref[:, ks(k)]
        mean = jnp.sum(block, axis=0, keepdims=True) * (1.0 / ph_dev)
        centered = block - mean
        stat[0, 0:1, ks(k)] = mean
        stat[0, 1:2, ks(k)] = jnp.sum(centered * centered, axis=0, keepdims=True)
        return carry

    lax.fori_loop(0, count, local_stats, 0)

    neighbours = jnp.where(me > 0, 1, 0) + jnp.where(me < n_space - 1, 1, 0)
    pl.semaphore_wait(barrier, rounds + neighbours)

    def plane_weights(k, carry):
        for axis, weights in ((0, wx), (1, wy)):
            corner, offset = split_coord(xy_ref[axis:axis + 1, ks(k)])
            weights[:, ks(k)] = spread(corner, offset, 0, GX)
        return carry

    for r in range(rounds):
        copy = pltpu.make_async_remote_copy(
            src_ref=stat.at[r],
            dst_ref=heard.at[r],
            send_sem=stat_send.at[r],
            recv_sem=stat_recv.at[r],
            device_id={"phase": partners[r]},
            device_id_type=MESH,
        )
        copy.start()
        lax.fori_loop(count * r // rounds, count * (r + 1) // rounds, plane_weights, 0)
        copy.wait()
        half = 0.5 * (ph_dev << r)

        def join(k, carry, r=r, half=half):
            apart = stat[r, 0:1, ks(k)] - heard[r, 0:1, ks(k)]
            stat[r + 1, 0:1, ks(k)] = 0.5 * (stat[r, 0:1, ks(k)] + heard[r, 0:1, ks(k)])
            stat[r + 1, 1:2, ks(k)] = (
                stat[r, 1:2, ks(k)] + heard[r, 1:2, ks(k)] + half * (apart * apart)
            )
            return carry

        lax.fori_loop(0, count, join, 0)

    def lift(k, carry):
        mean = stat[rounds, 0:1, ks(k)]
        var = stat[rounds, 1:2, ks(k)] * (1.0 / (ph_dev * n_phase))
        deviation = (inten_ref[:, ks(k)] - mean) * (2.0 * lax.rsqrt(var + 1.0))
        for c in range(3):
            forces[c * ph_dev:(c + 1) * ph_dev, :] = deviation * grad_ref[c, :, ks(k)].astype(
                jnp.float32
            )
        corner, offset = split_coord(z_ref[:, ks(k)])
        corner = corner + owner_ref[:, ks(k)] * GZ_DEV
        for o in range(n_space):
            along_z = spread(corner, offset, o * GZ_DEV, GZ_DEV)
            for pair in range(3 * ph_dev // 2):
                both = jnp.concatenate(
                    [
                        forces[2 * pair:2 * pair + 1, :] * along_z,
                        forces[2 * pair + 1:2 * pair + 2, :] * along_z,
                    ],
                    axis=0,
                )
                at = o * rows + 2 * pair * GZ_DEV
                lifted[at:at + 2 * GZ_DEV, ks(k)] = both.astype(jnp.bfloat16)
        return carry

    lax.fori_loop(0, count, lift, 0)

    def up_copy(c, j):
        return pltpu.make_async_remote_copy(
            src_ref=acc.at[c, n_space - 1 - j],
            dst_ref=from_low.at[c, j],
            send_sem=up_send.at[c, j],
            recv_sem=up_recv.at[c, j],
            device_id={"space": me + 1},
            device_id_type=MESH,
        )

    def down_copy(c, j):
        return pltpu.make_async_remote_copy(
            src_ref=acc.at[c, j],
            dst_ref=from_high.at[c, j],
            send_sem=down_send.at[c, j],
            recv_sem=down_recv.at[c, j],
            device_id={"space": me - 1},
            device_id_type=MESH,
        )

    def forward_up(c):
        def one(j, carry):
            target = n_space - 1 - j

            @pl.when((me > 0) & (me <= target))
            def _():
                up_copy(c, j).wait_recv()

            @pl.when((me > 0) & (me < target))
            def _():
                acc[c, target] += from_low[c, j]

            @pl.when(me < target)
            def _():
                up_copy(c, j).start()

            return carry

        lax.fori_loop(0, n_space - 1, one, 0)

    def forward_down(c):
        def one(j, carry):
            @pl.when((me < n_space - 1) & (me >= j))
            def _():
                down_copy(c, j).wait_recv()

            @pl.when((me < n_space - 1) & (me > j))
            def _():
                acc[c, j] += from_high[c, j]

            @pl.when(me > j)
            def _():
                down_copy(c, j).start()

            return carry

        lax.fori_loop(0, n_space - 1, one, 0)

    def slot(t, carry):
        @pl.when(t < chunks)
        def _():
            acc[t] = jnp.zeros(acc.shape[1:], jnp.float32)

            def multiply(k, inner):
                along_y = wy[:, mk(k)]
                along_x = wx[pl.ds(pl.multiple_of(t * X_STEP, X_STEP), X_STEP), mk(k)]
                plane = jnp.concatenate(
                    [(along_x[i:i + 1] * along_y).astype(jnp.bfloat16) for i in range(X_STEP)],
                    axis=0,
                )
                part = lax.dot_general(
                    lifted[:, mk(k)], plane, (((1,), (1,)), ((), ())),
                    preferred_element_type=jnp.float32,
                )
                acc[t] += part.reshape(n_space, rows, cols)
                return inner

            lax.fori_loop(0, samples // mstep, multiply, 0)

        c_up = t - me
        c_down = t - (n_space - 1 - me)

        @pl.when((c_up >= 0) & (c_up < chunks))
        def _():
            forward_up(c_up)

        @pl.when((c_down >= 0) & (c_down < chunks))
        def _():
            forward_down(c_down)

        return carry

    lax.fori_loop(0, chunks + n_space - 1, slot, 0)

    for c in range(chunks):
        out_ref[:, c * cols:(c + 1) * cols] = acc[c, me]

        @pl.when(me > 0)
        def _():
            out_ref[:, c * cols:(c + 1) * cols] += from_low[c, n_space - 1 - me]

        @pl.when(me < n_space - 1)
        def _():
            out_ref[:, c * cols:(c + 1) * cols] += from_high[c, me]

    def drain(j, carry):
        for c in range(chunks):
            @pl.when(me < n_space - 1 - j)
            def _():
                up_copy(c, j).wait_send()

            @pl.when(me > j)
            def _():
                down_copy(c, j).wait_send()

        return carry

    lax.fori_loop(0, n_space - 1, drain, 0)


def local(intensity, image_grad, owner, coord_xy, coord_z):
    ph_dev, samples = intensity.shape
    n_space = lax.axis_size("space")
    n_phase = lax.axis_size("phase")
    step = min(1024, samples)
    rows = 3 * ph_dev * GZ_DEV
    chunks = GX // X_STEP
    cols = X_STEP * GX
    rounds = n_phase.bit_length() - 1
    hops = n_space - 1
    dma = pltpu.SemaphoreType.DMA
    out = pl.pallas_call(
        functools.partial(kernel, n_space, n_phase, step),
        out_shape=jax.ShapeDtypeStruct((rows, GX * GX), jnp.float32),
        in_specs=[pl.BlockSpec(memory_space=pltpu.VMEM)] * 5,
        out_specs=pl.BlockSpec(memory_space=pltpu.VMEM),
        scratch_shapes=[
            pltpu.VMEM((rounds + 1, 2, samples), jnp.float32),
            pltpu.VMEM((rounds, 2, samples), jnp.float32),
            pltpu.VMEM((GX, samples), jnp.float32),
            pltpu.VMEM((GX, samples), jnp.float32),
            pltpu.VMEM((3 * ph_dev, step), jnp.float32),
            pltpu.VMEM((n_space * rows, samples), jnp.bfloat16),
            pltpu.VMEM((chunks, n_space, rows, cols), jnp.float32),
            pltpu.VMEM((chunks, hops, rows, cols), jnp.float32),
            pltpu.VMEM((chunks, hops, rows, cols), jnp.float32),
            dma((rounds,)),
            dma((rounds,)),
            dma((chunks, hops)),
            dma((chunks, hops)),
            dma((chunks, hops)),
            dma((chunks, hops)),
        ],
        compiler_params=pltpu.CompilerParams(
            collective_id=0, has_side_effects=True, vmem_limit_bytes=58 * 1024 * 1024
        ),
    )(
        intensity,
        image_grad,
        owner.reshape(1, samples),
        coord_xy,
        coord_z.reshape(1, samples),
    )
    return out.reshape(3, ph_dev, GZ_DEV, GX * GX)


def solution(mesh):
    return jax.shard_map(
        local,
        mesh=mesh,
        in_specs=(
            P("phase", ("groups", "space")),
            P(None, "phase", ("groups", "space")),
            P(("groups", "space"), None),
            P(None, ("groups", "space")),
            P(("groups", "space")),
        ),
        out_specs=P("groups", "phase", "space", None),
        check_vma=False,
    )
```

```python
import functools

import jax
import jax.numpy as jnp
from jax import lax
from jax.experimental import pallas as pl
from jax.experimental.pallas import tpu as pltpu
from jax.sharding import PartitionSpec as P

GX = 32
SPC = 16
GZ_DEV = 8
X_STEP = 8
MESH = pl.DeviceIdType.MESH


def spline_values(offset):
    square = offset * offset
    cube = square * offset
    remain = 1.0 - offset
    sixth = 1.0 / 6.0
    return (
        remain * remain * remain * sixth,
        (3.0 * cube - 6.0 * square + 4.0) * sixth,
        (-3.0 * cube + 3.0 * square + 3.0 * offset + 1.0) * sixth,
        cube * sixth,
    )


def spread(corner, offset, first, extent):
    width = corner.shape[1]
    row = first + lax.broadcasted_iota(jnp.int32, (extent, width), 0)
    distance = row - corner
    weights = jnp.zeros((extent, width), jnp.float32)
    for which, value in enumerate(spline_values(offset)):
        weights = jnp.where(distance == which, value, weights)
    return weights


def split_coord(coord):
    corner = coord // SPC
    return corner, (coord - corner * SPC).astype(jnp.float32) * (1.0 / SPC)


def kernel(
    n_space, n_phase, step,
    inten_ref, grad_ref, owner_ref, xy_ref, z_ref, out_ref,
    stat, heard, wx, wy, forces, lifted, acc, from_low, from_high,
    stat_send, stat_recv, up_send, up_recv, down_send, down_recv,
):
    ph_dev, samples = inten_ref.shape
    count = samples // step
    rows = 3 * ph_dev * GZ_DEV
    chunks = GX // X_STEP
    cols = X_STEP * GX
    rounds = n_phase.bit_length() - 1
    me = lax.axis_index("space")
    ph = lax.axis_index("phase")
    partners = [ph + (1 - 2 * ((ph // (1 << r)) % 2)) * (1 << r) for r in range(rounds)]

    barrier = pltpu.get_barrier_semaphore()
    for partner in partners:
        pl.semaphore_signal(barrier, inc=1, device_id={"phase": partner}, device_id_type=MESH)

    @pl.when(me > 0)
    def _():
        pl.semaphore_signal(barrier, inc=1, device_id={"space": me - 1}, device_id_type=MESH)

    @pl.when(me < n_space - 1)
    def _():
        pl.semaphore_signal(barrier, inc=1, device_id={"space": me + 1}, device_id_type=MESH)

    def ks(k):
        return pl.ds(k * step if isinstance(k, int) else pl.multiple_of(k * step, step), step)

    mstep = min(4096, samples)

    def mk(k):
        return pl.ds(k * mstep if isinstance(k, int) else pl.multiple_of(k * mstep, mstep), mstep)

    def local_stats(k, carry):
        block = inten_ref[:, ks(k)]
        mean = jnp.sum(block, axis=0, keepdims=True) * (1.0 / ph_dev)
        centered = block - mean
        stat[0, 0:1, ks(k)] = mean
        stat[0, 1:2, ks(k)] = jnp.sum(centered * centered, axis=0, keepdims=True)
        return carry

    lax.fori_loop(0, count, local_stats, 0)

    neighbours = jnp.where(me > 0, 1, 0) + jnp.where(me < n_space - 1, 1, 0)
    pl.semaphore_wait(barrier, rounds + neighbours)

    def plane_weights(k, carry):
        for axis, weights in ((0, wx), (1, wy)):
            corner, offset = split_coord(xy_ref[axis:axis + 1, ks(k)])
            weights[:, ks(k)] = spread(corner, offset, 0, GX)
        return carry

    for r in range(rounds):
        copy = pltpu.make_async_remote_copy(
            src_ref=stat.at[r],
            dst_ref=heard.at[r],
            send_sem=stat_send.at[r],
            recv_sem=stat_recv.at[r],
            device_id={"phase": partners[r]},
            device_id_type=MESH,
        )
        copy.start()
        lax.fori_loop(count * r // rounds, count * (r + 1) // rounds, plane_weights, 0)
        copy.wait()
        half = 0.5 * (ph_dev << r)

        def join(k, carry, r=r, half=half):
            apart = stat[r, 0:1, ks(k)] - heard[r, 0:1, ks(k)]
            stat[r + 1, 0:1, ks(k)] = 0.5 * (stat[r, 0:1, ks(k)] + heard[r, 0:1, ks(k)])
            stat[r + 1, 1:2, ks(k)] = (
                stat[r, 1:2, ks(k)] + heard[r, 1:2, ks(k)] + half * (apart * apart)
            )
            return carry

        lax.fori_loop(0, count, join, 0)

    def lift(k, carry):
        mean = stat[rounds, 0:1, ks(k)]
        var = stat[rounds, 1:2, ks(k)] * (1.0 / (ph_dev * n_phase))
        deviation = (inten_ref[:, ks(k)] - mean) * (2.0 * lax.rsqrt(var + 1.0))
        for c in range(3):
            forces[c * ph_dev:(c + 1) * ph_dev, :] = deviation * grad_ref[c, :, ks(k)].astype(
                jnp.float32
            )
        corner, offset = split_coord(z_ref[:, ks(k)])
        corner = corner + owner_ref[:, ks(k)] * GZ_DEV
        for o in range(n_space):
            along_z = spread(corner, offset, o * GZ_DEV, GZ_DEV)
            for pair in range(3 * ph_dev // 2):
                both = jnp.concatenate(
                    [
                        forces[2 * pair:2 * pair + 1, :] * along_z,
                        forces[2 * pair + 1:2 * pair + 2, :] * along_z,
                    ],
                    axis=0,
                )
                at = o * rows + 2 * pair * GZ_DEV
                lifted[at:at + 2 * GZ_DEV, ks(k)] = both.astype(jnp.bfloat16)
        return carry


    def up_copy(c, j):
        return pltpu.make_async_remote_copy(
            src_ref=acc.at[c, n_space - 1 - j],
            dst_ref=from_low.at[c, j],
            send_sem=up_send.at[c, j],
            recv_sem=up_recv.at[c, j],
            device_id={"space": me + 1},
            device_id_type=MESH,
        )

    def down_copy(c, j):
        return pltpu.make_async_remote_copy(
            src_ref=acc.at[c, j],
            dst_ref=from_high.at[c, j],
            send_sem=down_send.at[c, j],
            recv_sem=down_recv.at[c, j],
            device_id={"space": me - 1},
            device_id_type=MESH,
        )

    top = n_space - 1

    def step_up(c, j):
        target = top - j

        @pl.when((me > 0) & (me < target))
        def _():
            up_copy(c, j).wait_recv()
            acc[c, target] += from_low[c, j]

        @pl.when(me < target)
        def _():
            up_copy(c, j).start()

    def step_down(c, j):
        @pl.when((me < top) & (me > j))
        def _():
            down_copy(c, j).wait_recv()
            acc[c, j] += from_high[c, j]

        @pl.when(me > j)
        def _():
            down_copy(c, j).start()

    def forward_up(c):
        def one(j, carry):
            @pl.when(me < top - j - 1)
            def _():
                step_up(c, j)

            return carry

        lax.fori_loop(0, top - 1, one, 0)

    def forward_down(c):
        def one(j, carry):
            @pl.when(me > j + 1)
            def _():
                step_down(c, j)

            return carry

        lax.fori_loop(0, top - 1, one, 0)

    def multiply_chunk(t, k):
        along_y = wy[:, mk(k)]
        along_x = wx[pl.ds(t * X_STEP if isinstance(t, int) else pl.multiple_of(t * X_STEP, X_STEP), X_STEP), mk(k)]
        plane = jnp.concatenate(
            [(along_x[i:i + 1] * along_y).astype(jnp.bfloat16) for i in range(X_STEP)],
            axis=0,
        )
        part = lax.dot_general(
            lifted[:, mk(k)], plane, (((1,), (1,)), ((), ())),
            preferred_element_type=jnp.float32,
        )
        acc[t] += part.reshape(n_space, rows, cols)

    acc[0] = jnp.zeros(acc.shape[1:], jnp.float32)
    per = mstep // step
    for k in range(samples // mstep + 1):
        if k < samples // mstep:
            for kk in range(k * per, (k + 1) * per):
                lift(kk, 0)
        if k > 0:
            multiply_chunk(0, k - 1)

    def slot(t, carry):
        @pl.when((t > 0) & (t < chunks))
        def _():
            def multiply(k, inner):
                multiply_chunk(t, k)
                return inner

            acc[t] = jnp.zeros(acc.shape[1:], jnp.float32)
            lax.fori_loop(0, samples // mstep, multiply, 0)

        c_up = t - me
        c_down = t - (n_space - 1 - me)

        @pl.when((c_up >= 0) & (c_up < chunks))
        def _():
            forward_up(c_up)

        @pl.when((c_down >= 0) & (c_down < chunks))
        def _():
            forward_down(c_down)

        return carry

    lax.fori_loop(0, chunks + n_space - 1, slot, 0)

    def last_hop(c, carry):
        @pl.when(me < top)
        def _():
            step_up(c, top - 1 - me)

        @pl.when(me > 0)
        def _():
            step_down(c, me - 1)

        return carry

    lax.fori_loop(0, chunks, last_hop, 0)

    for c in range(chunks):
        out_ref[:, c * cols:(c + 1) * cols] = acc[c, me]

        @pl.when(me > 0)
        def _():
            up_copy(c, n_space - 1 - me).wait_recv()
            out_ref[:, c * cols:(c + 1) * cols] += from_low[c, n_space - 1 - me]

        @pl.when(me < n_space - 1)
        def _():
            down_copy(c, me).wait_recv()
            out_ref[:, c * cols:(c + 1) * cols] += from_high[c, me]

    def drain(j, carry):
        for c in range(chunks):
            @pl.when(me < n_space - 1 - j)
            def _():
                up_copy(c, j).wait_send()

            @pl.when(me > j)
            def _():
                down_copy(c, j).wait_send()

        return carry

    lax.fori_loop(0, n_space - 1, drain, 0)


def local(intensity, image_grad, owner, coord_xy, coord_z):
    ph_dev, samples = intensity.shape
    n_space = lax.axis_size("space")
    n_phase = lax.axis_size("phase")
    step = min(1024, samples)
    rows = 3 * ph_dev * GZ_DEV
    chunks = GX // X_STEP
    cols = X_STEP * GX
    rounds = n_phase.bit_length() - 1
    hops = n_space - 1
    dma = pltpu.SemaphoreType.DMA
    out = pl.pallas_call(
        functools.partial(kernel, n_space, n_phase, step),
        out_shape=jax.ShapeDtypeStruct((rows, GX * GX), jnp.float32),
        in_specs=[pl.BlockSpec(memory_space=pltpu.VMEM)] * 5,
        out_specs=pl.BlockSpec(memory_space=pltpu.VMEM),
        scratch_shapes=[
            pltpu.VMEM((rounds + 1, 2, samples), jnp.float32),
            pltpu.VMEM((rounds, 2, samples), jnp.float32),
            pltpu.VMEM((GX, samples), jnp.float32),
            pltpu.VMEM((GX, samples), jnp.float32),
            pltpu.VMEM((3 * ph_dev, step), jnp.float32),
            pltpu.VMEM((n_space * rows, samples), jnp.bfloat16),
            pltpu.VMEM((chunks, n_space, rows, cols), jnp.float32),
            pltpu.VMEM((chunks, hops, rows, cols), jnp.float32),
            pltpu.VMEM((chunks, hops, rows, cols), jnp.float32),
            dma((rounds,)),
            dma((rounds,)),
            dma((chunks, hops)),
            dma((chunks, hops)),
            dma((chunks, hops)),
            dma((chunks, hops)),
        ],
        compiler_params=pltpu.CompilerParams(
            collective_id=0, has_side_effects=True, vmem_limit_bytes=58 * 1024 * 1024
        ),
    )(
        intensity,
        image_grad,
        owner.reshape(1, samples),
        coord_xy,
        coord_z.reshape(1, samples),
    )
    return out.reshape(3, ph_dev, GZ_DEV, GX * GX)


def solution(mesh):
    return jax.shard_map(
        local,
        mesh=mesh,
        in_specs=(
            P("phase", ("groups", "space")),
            P(None, "phase", ("groups", "space")),
            P(("groups", "space"), None),
            P(None, ("groups", "space")),
            P(("groups", "space")),
        ),
        out_specs=P("groups", "phase", "space", None),
        check_vma=False,
    )
```
